512 devices in a mesh: grp: 16 (over z), dev: 32 (over y, x, core).
Axes of the slice: x: 4, y: 4, z: 16, core: 2. Of those that a mesh axis runs over, the one named last changes fastest.
Arguments:
- signals: bfloat16 [192, 96, 256, 256], P(None, 'grp', 'dev'), may hold values from -17 to 17
- tile_flags: int32 [96, 256, 2], P('grp', 'dev'), may hold values 0 or 1
- basis_old: float32 [192, 8], replicated, may hold values from -6 to 6
- tv_weight: float32 [96, 256, 256], P('grp', 'dev'), may hold values from 0.2 to 2
Outputs:
- basis: float32 [192, 8], replicated
- coefficients: float32 [8, 96, 256, 256], P(None, 'grp', 'dev')
The draws below stay inside these ranges and needn't reach their ends.
All inputs are finite; a program needn't handle non-finite values. No bound on the sum of `tile_flags` on one device may be relied on, other than what follows from the above.
Results may differ from the reference program's by a relative error of at most 0.002.
Values sent between devices are 32-bit elements; how exact they have to be, the bound alone decides.
No kernel may reach another device: no remote copies, remote signals or barrier semaphores. Data moves between devices by JAX's collectives and lax.ppermute only.
A program may use at most 64 MiB of HBM per device.

```python
import math
import jax
import jax.numpy as jnp
from jax import lax

F = 192
R = 8
TILE = 128
CZ = 256
NX = 96
NY = 256


curve_count = 24


def draw_signals(key, part):
    key = jax.random.fold_in(key, 11)
    keys = jax.random.split(key, 8)
    frame = jnp.arange(F, dtype=jnp.float32)[:, None, None, None]
    xpos = (2.0 * jnp.arange(NX, dtype=jnp.float32) / (NX - 1) - 1.0)[None, :, None, None]
    ypos = (2.0 * jnp.arange(NY, dtype=jnp.float32) / (NY - 1) - 1.0)[None, None, :, None]
    rise = 1.0 + 2.0 * jnp.arange(NX, dtype=jnp.float32)[None, :, None, None] / (NX - 1)
    times = jnp.exp(jax.random.uniform(keys[0], (curve_count,), jnp.float32, math.log(0.03), math.log(0.6)))
    waves = (jnp.arange(curve_count, dtype=jnp.float32) + 1.0 + jax.random.uniform(keys[1], (curve_count,), jnp.float32, 0.0, 0.5)) * math.pi / F
    phases = jax.random.uniform(keys[2], (curve_count,), jnp.float32, -math.pi, math.pi)
    slope_x = jax.random.uniform(keys[3], (curve_count,), jnp.float32, -0.8, 0.8)
    slope_y = jax.random.uniform(keys[4], (curve_count,), jnp.float32, -0.8, 0.8)
    weights = jnp.clip(jax.random.normal(keys[5], (curve_count, NX, NY, CZ), jnp.float32), -4.0, 4.0)
    noise = 0.1 * jnp.clip(jax.random.normal(keys[6], (F, NX, NY, CZ), jnp.float32), -4.0, 4.0)
    spread = jnp.exp(jax.random.uniform(keys[7], (1, NX, NY, 1), jnp.float32, -1.15, 1.15))
    inner = noise
    for index in range(curve_count):
        curve = (1.0 - 1.6 * jnp.exp(-(frame + 1.0) / (F * times[index]))) * jnp.cos(waves[index] * frame + phases[index])
        amplitude = 0.43 * 10.0 ** (-index / (curve_count - 1))
        region = jnp.exp(slope_x[index] * xpos + slope_y[index] * ypos)
        inner = inner + curve * (amplitude * region * weights[index][None])
    return jnp.clip(inner * spread * rise / 3.0, -16.0, 16.0).astype(jnp.bfloat16)


def set_ends(values, own_key, low, top_value):
    longest = values.shape.index(max(values.shape))
    spots = []
    for shift in (0, 1):
        where = [jax.random.randint(jax.random.fold_in(own_key, axis), (), 0, length) for axis, length in enumerate(values.shape)]
        where[longest] = (where[longest] + shift) % values.shape[longest]
        spots.append(tuple(where))
    return values.at[spots[0]].set(low).at[spots[1]].set(top_value)


def block_levels(stream_key, shape, cuts, low, top_value):
    factor_of, own = 1.0, jax.random.fold_in(stream_key, 6)
    for dim, parts in cuts:
        steps = jnp.exp(jax.random.uniform(jax.random.fold_in(own, dim), (parts,), jnp.float32, low / len(cuts), top_value / len(cuts)))
        factor_of = factor_of * jnp.repeat(steps, shape[dim] // parts).reshape([-1 if axis == dim else 1 for axis in range(len(shape))])
    return factor_of


def normal_values(key, extent, deviation, limit, held_as=jnp.bfloat16):
    array = jax.random.normal(key, extent, jnp.float32) * deviation
    return jnp.minimum(jnp.maximum(array, -limit), limit).astype(held_as)


def setup_inputs(seed: int = 0) -> dict:
    splits = jax.random.split(jax.random.key(seed), 5)
    signals = draw_signals(jax.random.fold_in(splits[4], 71), 0)
    tile_flags = set_ends((jax.random.randint(splits[1], (NX, NY, CZ // TILE), 0, 4) < 3).astype(jnp.int32), jax.random.fold_in(splits[1], 1), 0, 1)
    basis_old = normal_values(splits[2], (F, R), 1.0, 6.0, jnp.float32)
    tv_weight = jnp.clip(jnp.exp(math.log(2.0) - 2.3025851 * jax.random.uniform(splits[3], (NX, NY, CZ), jnp.float32) ** block_levels(splits[3], (NX, NY, CZ), ((0, 16), (1, 32)), -0.2, 0.2)), 0.2, 2.0)
    return {"signals": signals, "tile_flags": tile_flags, "basis_old": basis_old, "tv_weight": tv_weight}


step_size = 0.08

def tv_update(extended, weight):
    zpad = jnp.pad(extended, ((0, 0), (0, 0), (0, 0), (1, 1)))
    center = zpad[:, 1:-1, 1:-1, 1:-1]
    neighbours = [zpad[:, 2:, 1:-1, 1:-1], zpad[:, :-2, 1:-1, 1:-1], zpad[:, 1:-1, 2:, 1:-1], zpad[:, 1:-1, :-2, 1:-1], zpad[:, 1:-1, 1:-1, 2:], zpad[:, 1:-1, 1:-1, :-2]]
    total = jnp.zeros_like(center)
    for other in neighbours:
        diff = other - center
        total = total + diff / jnp.sqrt(1.0 + diff * diff)
    return center + step_size * weight * total

def orthonormal(grown):
    small = jnp.dot(grown.T, grown, precision=lax.Precision.HIGHEST)
    lower = jnp.linalg.cholesky(small)
    return lax.linalg.triangular_solve(lower, grown, left_side=False, lower=True, transpose_a=True)

def reference(signals, tile_flags, basis_old, tv_weight):
    flags = jnp.repeat(tile_flags, TILE, axis=2).astype(jnp.bfloat16)
    masked = signals * flags[None]

    def gram_slice(carry, piece):
        flat = piece.reshape(F, -1).astype(jnp.float32)
        return (carry + jnp.dot(flat, flat.T, precision=lax.Precision.HIGHEST), None)
    gram, _ = lax.scan(gram_slice, jnp.zeros((F, F), jnp.float32), jnp.moveaxis(masked, 1, 0))
    grown = jnp.dot(gram, basis_old, precision=lax.Precision.HIGHEST)
    basis = orthonormal(grown)

    def project_slice(piece):
        return jnp.einsum('fyz,fr->ryz', piece.astype(jnp.float32), basis, precision=lax.Precision.HIGHEST)
    projected = jnp.moveaxis(lax.map(project_slice, jnp.moveaxis(masked, 1, 0)), 0, 1)
    coef = projected
    for sweep in range(2):
        extended = jnp.pad(coef, ((0, 0), (1, 1), (1, 1), (0, 0)))
        coef = tv_update(extended, tv_weight)
    return (basis, coef)
```

```python
import functools

import jax
import jax.numpy as jnp
import numpy as np
from jax import lax
from jax.experimental import pallas as pl
from jax.experimental.pallas import tpu as pltpu
from jax.sharding import PartitionSpec as P

step_size = 0.08
limit = 40 * 1024 * 1024
NT = (((1,), (1,)), ((), ()))
TN = (((0,), (0,)), ((), ()))


def dot(a, b, dims=(((1,), (0,)), ((), ()))):
    return lax.dot_general(a, b, dims, preferred_element_type=jnp.float32)


def terms(values, count):
    parts = []
    for _ in range(count):
        part = values.astype(jnp.bfloat16)
        parts.append(part)
        values = values - part.astype(jnp.float32)
    return parts


def spread_rows(repeated, rows):
    lane = lax.broadcasted_iota(jnp.int32, repeated.shape, 1) % rows
    return [jnp.where(lane == y, repeated, 0.0) for y in range(rows)]


def to_dense(values):
    rest = values[:, 128:]
    tail = jnp.concatenate([rest[:4], rest[4:]], axis=1)
    return jnp.stack([values[:4, :128], values[4:, :128], tail])


def from_dense(values):
    first = jnp.concatenate([values[0], values[1]], axis=0)
    rest = jnp.concatenate([values[2, :, :64], values[2, :, 64:]], axis=0)
    return jnp.concatenate([first, rest], axis=1)


def tile_mask(flags, width, tiles):
    return jnp.concatenate([jnp.broadcast_to(flags[:, t : t + 1], (flags.shape[0], width)) for t in range(tiles)], axis=1)


def load_planes(signals, planes, sems):
    copies = [
        pltpu.make_async_copy(signals.at[:, i], planes.at[i], sems.at[i]) for i in range(planes.shape[0])
    ]
    for copy in copies:
        copy.start()
    return copies


def rows_of(plane):
    frames, rows, width = plane.shape
    return plane.astype(jnp.float32).reshape(frames * rows, width).astype(jnp.bfloat16)


def grown_kernel(signals, flags, basis_old, select, out, planes, sems):
    copies = load_planes(signals, planes, sems)
    count, frames, rows, width = planes.shape
    rank = basis_old.shape[1]
    spread = []
    for part in terms(basis_old[...], 3):
        spread += spread_rows(dot(part, select[...], TN), rows)
    weights = jnp.concatenate(spread, axis=0).astype(jnp.bfloat16)
    total = jnp.zeros((rows * rank, frames * rows), jnp.float32)
    for i in range(count):
        copies[i].wait()
        flat = rows_of(planes[i])
        mixed = dot(weights, flat).reshape(3, rows * rank, width).sum(0)
        keep = tile_mask(flags[i].astype(jnp.float32), width // flags.shape[2], flags.shape[2])
        mixed = (mixed.reshape(rows, rank, width) * keep[:, None, :]).reshape(rows * rank, width)
        product = dot(jnp.concatenate(terms(mixed, 3), axis=0), flat, NT)
        total = total + product.reshape(3, rows * rank, frames * rows).sum(0)
    total = total.reshape(rows, rank, frames * rows)
    lane = lax.broadcasted_iota(jnp.int32, (rank, frames * rows), 1) % rows
    diagonal = jnp.zeros((rank, frames * rows), jnp.float32)
    for y in range(rows):
        diagonal = diagonal + jnp.where(lane == y, total[y], 0.0)
    grown = dot(jnp.concatenate(terms(diagonal, 3), axis=0), select[...], NT)
    grown = grown.reshape(3, rank, frames).sum(0)
    out[...] = jnp.broadcast_to(to_dense(grown)[None], out.shape)


def local_grown(signals, tile_flags, basis_old, select, copies):
    frames, size_x, size_y, size_z = signals.shape
    return pl.pallas_call(
        grown_kernel,
        out_shape=jax.ShapeDtypeStruct((copies, 3, 4, 128), jnp.float32),
        in_specs=[pl.BlockSpec(memory_space=pl.ANY)] + [pl.BlockSpec(memory_space=pltpu.VMEM)] * 3,
        out_specs=pl.BlockSpec(memory_space=pltpu.VMEM),
        scratch_shapes=[
            pltpu.VMEM((size_x, frames, size_y, size_z), signals.dtype),
            pltpu.SemaphoreType.DMA((size_x,)),
        ],
        compiler_params=pltpu.CompilerParams(vmem_limit_bytes=limit),
        name="local_grown",
    )(signals, tile_flags, basis_old, select)


def resend_kernel(parts, out):
    out[...] = jnp.broadcast_to(jnp.sum(parts[...], axis=0, keepdims=True), out.shape)


def sum_and_copy(parts, copies):
    return pl.pallas_call(
        resend_kernel,
        out_shape=jax.ShapeDtypeStruct((copies,) + parts.shape[1:], jnp.float32),
        in_specs=[pl.BlockSpec(memory_space=pltpu.VMEM)],
        out_specs=pl.BlockSpec(memory_space=pltpu.VMEM),
        name="sum_and_copy",
    )(parts)


def orthonormal(grown):
    rank = grown.shape[0]
    row = lax.broadcasted_iota(jnp.int32, (rank, 1), 0)
    for k in range(rank):
        pivot = grown[k : k + 1]
        inner = jnp.sum(grown * pivot, axis=1, keepdims=True)
        norm2 = inner[k : k + 1]
        scaled = pivot * (1.0 / norm2)
        grown = jnp.where(row > k, grown - inner * scaled, grown)
        grown = jnp.where(row == k, pivot / jnp.sqrt(norm2), grown)
    return grown


def project_kernel(parts, signals, flags, select, weight, basis_out, coef, head, tail, planes, sems):
    copies = load_planes(signals, planes, sems)
    count, frames, rows, width = planes.shape
    basis = orthonormal(from_dense(jnp.sum(parts[...], axis=0)))
    rank = basis.shape[0]
    basis_out[...] = basis
    spread = []
    for part in terms(basis, 2):
        spread += spread_rows(dot(part, select[...]), rows)
    weights = jnp.concatenate(spread, axis=0).astype(jnp.bfloat16)
    for i in range(count):
        copies[i].wait()
        mixed = dot(weights, rows_of(planes[i])).reshape(2, rows, rank, width).sum(0)
        keep = tile_mask(flags[i].astype(jnp.float32), width // flags.shape[2], flags.shape[2])
        mixed = mixed * keep[:, None, :]
        coef[i] = mixed
        for y in range(2):
            head[y * count + i] = mixed[y]
            tail[y * count + i] = mixed[rows - 2 + y]
    head[2 * count, :count] = weight[:, 0]
    tail[2 * count, :count] = weight[:, rows - 1]
    head[2 * count, count:] = jnp.zeros((rank - count, width), jnp.float32)
    tail[2 * count, count:] = jnp.zeros((rank - count, width), jnp.float32)


def project(parts, signals, tile_flags, select, tv_weight, rank):
    frames, size_x, size_y, size_z = signals.shape
    edge = jax.ShapeDtypeStruct((2 * size_x + 1, rank, size_z), jnp.float32)
    vmem = pl.BlockSpec(memory_space=pltpu.VMEM)
    return pl.pallas_call(
        project_kernel,
        out_shape=(
            jax.ShapeDtypeStruct((rank, frames), jnp.float32),
            jax.ShapeDtypeStruct((size_x, size_y, rank, size_z), jnp.float32),
            edge,
            edge,
        ),
        in_specs=[vmem, pl.BlockSpec(memory_space=pl.ANY), vmem, vmem, vmem],
        out_specs=(vmem,) * 4,
        scratch_shapes=[
            pltpu.VMEM((size_x, frames, size_y, size_z), signals.dtype),
            pltpu.SemaphoreType.DMA((size_x,)),
        ],
        compiler_params=pltpu.CompilerParams(vmem_limit_bytes=limit),
        name="project",
    )(parts, signals, tile_flags, select, tv_weight)


def slope(diff):
    return diff * lax.rsqrt(1.0 + diff * diff)


def along_z(cells):
    width = cells.shape[-1]
    lane = lax.broadcasted_iota(jnp.int32, cells.shape, cells.ndim - 1)
    above = jnp.where(lane == width - 1, 0.0, pltpu.roll(cells, width - 1, cells.ndim - 1))
    flux = slope(above - cells)
    below = jnp.where(lane == 0, slope(cells), pltpu.roll(flux, 1, cells.ndim - 1))
    return flux - below


def smooth_kernel(coef, left, right, down, up, weight, out, first, second, weights):
    count, rows, rank, width = coef.shape
    planes = count + 4
    lo, hi = slice(2, 2 + rows), slice(1, 3 + rows)
    first[0, lo] = down[:rows]
    first[1, hi] = down[rows : 2 * rows + 2]
    first[planes - 1, lo] = up[:rows]
    first[planes - 2, hi] = up[rows : 2 * rows + 2]
    first[2 : 2 + count, lo] = coef[...]
    for y in range(2):
        first[2 : 2 + count, y] = left[y * count : (y + 1) * count]
        first[2 : 2 + count, 2 + rows + y] = right[y * count : (y + 1) * count]
    weights[1 : 1 + count, 1 : 1 + rows] = weight[...]
    weights[1 : 1 + count, 0] = left[2 * count, :count]
    weights[1 : 1 + count, 1 + rows] = right[2 * count, :count]
    weights[0, 1 : 1 + rows] = down[2 * rows + 2]
    weights[1 + count, 1 : 1 + rows] = up[2 * rows + 2]

    def update(field, i, ys, size, before, wrow):
        cells = field[i, ys : ys + size]
        after = slope(field[i + 1, ys : ys + size] - cells)
        sides = slope(field[i, ys : ys + size + 1] - field[i, ys - 1 : ys + size])
        total = (after - before) + (sides[1:] - sides[:-1]) + along_z(cells)
        return cells + step_size * wrow[:, None, :] * total, after

    before = slope(first[1, lo] - first[0, lo])
    for i in range(1, planes - 1):
        edge = i == 1 or i == planes - 2
        ys, size = (2, rows) if edge else (1, rows + 2)
        if i == 2:
            before = slope(first[2, hi] - first[1, hi])
        if i == planes - 2:
            before = before[1 : 1 + rows]
        fresh, before = update(first, i, ys, size, before, weights[i - 1, ys - 1 : ys - 1 + size])
        second[i - 1, ys - 1 : ys - 1 + size] = fresh
    before = slope(second[1, 1 : 1 + rows] - second[0, 1 : 1 + rows])
    for i in range(1, count + 1):
        fresh, before = update(second, i, 1, rows, before, weights[i, 1 : 1 + rows])
        for y in range(rows):
            out[:, i - 1, y] = fresh[y]


def smooth(coef, left, right, down, up, tv_weight):
    count, rows, rank, width = coef.shape
    vmem = pl.BlockSpec(memory_space=pltpu.VMEM)
    return pl.pallas_call(
        smooth_kernel,
        out_shape=jax.ShapeDtypeStruct((rank, count, rows, width), jnp.float32),
        in_specs=[vmem] * 6,
        out_specs=vmem,
        scratch_shapes=[
            pltpu.VMEM((count + 4, rows + 4, rank, width), jnp.float32),
            pltpu.VMEM((count + 2, rows + 2, rank, width), jnp.float32),
            pltpu.VMEM((count + 2, rows + 2, width), jnp.float32),
        ],
        compiler_params=pltpu.CompilerParams(vmem_limit_bytes=limit),
        name="smooth",
    )(coef, left, right, down, up, tv_weight)


def neighbours(axis, toward_low, toward_high):
    ends = lax.axis_size(axis) - 1
    return (
        lax.ppermute(toward_high, axis, [(i, i + 1) for i in range(ends)]),
        lax.ppermute(toward_low, axis, [(i + 1, i) for i in range(ends)]),
    )


def on_device(signals, tile_flags, basis_old, tv_weight):
    frames, size_x, size_y, size_z = signals.shape
    rank = basis_old.shape[1]
    select = jnp.asarray(np.repeat(np.eye(frames), size_y, axis=1), jnp.bfloat16)
    parts = local_grown(signals, tile_flags, basis_old, select, lax.axis_size("grp"))
    parts = lax.all_to_all(parts, "grp", 0, 0)
    parts = sum_and_copy(parts, lax.axis_size("dev"))
    parts = lax.all_to_all(parts, "dev", 0, 0)
    basis, coef, head, tail = project(parts, signals, tile_flags, select, tv_weight, rank)
    left, right = neighbours("dev", head, tail)

    def face(far, near):
        return jnp.concatenate(
            [
                coef[far],
                left[size_x + near][None],
                coef[near],
                right[near][None],
                tv_weight[near][None],
            ],
            axis=0,
        )

    down, up = neighbours("grp", face(1, 0), face(size_x - 2, size_x - 1))
    return (basis.T, smooth(coef, left, right, down, up, tv_weight))


def solution(mesh):
    placed = (P(None, "grp", "dev", None), P("grp", "dev", None), P(), P("grp", "dev", None))
    return jax.shard_map(
        on_device,
        mesh=mesh,
        in_specs=placed,
        out_specs=(P(), P(None, "grp", "dev", None)),
        check_vma=False,
    )
```

```python
import jax
import jax.numpy as jnp
from jax import lax
from jax.experimental import pallas as pl
from jax.experimental.pallas import tpu as pltpu
from jax.sharding import PartitionSpec as P

step_size = 0.08
limit = 44 * 1024 * 1024
ahead = 3
held = 3
NT = (((1,), (1,)), ((), ()))
TN = (((0,), (0,)), ((), ()))


def dot(a, b, dims=(((1,), (0,)), ((), ()))):
    return lax.dot_general(a, b, dims, preferred_element_type=jnp.float32)


def terms(values, count):
    parts = []
    for _ in range(count):
        part = values.astype(jnp.bfloat16)
        parts.append(part)
        values = values - part.astype(jnp.float32)
    return parts


def spread_rows(repeated, rows):
    lane = lax.broadcasted_iota(jnp.int32, repeated.shape, 1) % rows
    return [jnp.where(lane == y, repeated, 0.0) for y in range(rows)]


def to_dense(values):
    rest = values[:, 128:]
    tail = jnp.concatenate([rest[:4], rest[4:]], axis=1)
    return jnp.stack([values[:4, :128], values[4:, :128], tail])


def from_dense(values):
    first = jnp.concatenate([values[0], values[1]], axis=0)
    rest = jnp.concatenate([values[2, :, :64], values[2, :, 64:]], axis=0)
    return jnp.concatenate([first, rest], axis=1)


def frame_select(frames, rows):
    shape = (frames, frames * rows)
    lane = lax.broadcasted_iota(jnp.int32, shape, 1) // rows
    return (lane == lax.broadcasted_iota(jnp.int32, shape, 0)).astype(jnp.bfloat16)


def tile_masks(flags, width):
    tiles = flags.shape[1]
    shape = (tiles, width)
    lane = lax.broadcasted_iota(jnp.int32, shape, 1) // (width // tiles)
    spread = (lane == lax.broadcasted_iota(jnp.int32, shape, 0)).astype(jnp.bfloat16)
    return [dot(flags[x].astype(jnp.bfloat16), spread, TN)[:, None, :] for x in range(flags.shape[0])]


def plane_refs(kept, spare):
    return [kept.at[i] for i in range(kept.shape[0])] + [spare.at[i] for i in range(spare.shape[0])]


def rows_of(plane):
    frames, rows, width = plane.shape
    return plane.reshape(frames * rows, width)


def mixing(rows_by_frame, select, count, rows):
    spread = []
    for part in terms(rows_by_frame, count):
        spread += spread_rows(dot(part, select), rows)
    return jnp.concatenate(spread, axis=0).astype(jnp.bfloat16)


def grown_kernel(signals, flags_in, basis_in, out, kept, spare, flags, basis_old, sems, small):
    first = [
        pltpu.make_async_copy(basis_in, basis_old, small.at[0]),
        pltpu.make_async_copy(flags_in, flags, small.at[1]),
    ]
    for copy in first:
        copy.start()
    frames, count, rows, width = signals.shape
    planes = plane_refs(kept, spare)
    copies = [pltpu.make_async_copy(signals.at[:, i], planes[i], sems.at[i]) for i in range(count)]
    for i in range(ahead):
        copies[i].start(priority=i % 2)
    rank = basis_old.shape[0]
    select = frame_select(frames, rows)
    for copy in first:
        copy.wait()
    weights = mixing(basis_old[...], select, 3, rows)
    keep = tile_masks(flags, width)

    def mix(i):
        copies[i].wait()
        if i + ahead < count:
            copies[i + ahead].start(priority=(i + ahead) % 2)
        flat = rows_of(planes[i][...])
        mixed = dot(weights, flat).reshape(3, rows, rank, width).sum(0) * keep[i]
        return jnp.concatenate(terms(mixed.reshape(rows * rank, width), 3), axis=0), flat

    def product(mixed, flat):
        return dot(mixed, flat, NT).reshape(3, rows, rank, frames * rows).sum(0)

    before = mix(0)
    total = jnp.zeros((rows, rank, frames * rows), jnp.float32)
    for i in range(1, count):
        now = mix(i)
        total = total + product(*before)
        before = now
    total = total + product(*before)
    lane = lax.broadcasted_iota(jnp.int32, (rank, frames * rows), 1) % rows
    diagonal = jnp.zeros((rank, frames * rows), jnp.float32)
    for y in range(rows):
        diagonal = diagonal + jnp.where(lane == y, total[y], 0.0)
    grown = dot(jnp.concatenate(terms(diagonal, 3), axis=0), select, NT)
    grown = grown.reshape(3, rank, frames).sum(0)
    out[...] = jnp.broadcast_to(to_dense(grown)[None], out.shape)


def local_grown(signals, flags, basis_old, copies):
    frames, size_x, size_y, size_z = signals.shape
    return pl.pallas_call(
        grown_kernel,
        out_shape=(
            jax.ShapeDtypeStruct((copies, 3, 4, 128), jnp.float32),
            jax.ShapeDtypeStruct((held, frames, size_y, size_z), signals.dtype),
        ),
        in_specs=[pl.BlockSpec(memory_space=pltpu.HBM)] * 3,
        out_specs=[pl.BlockSpec(memory_space=pltpu.VMEM)] * 2,
        scratch_shapes=[
            pltpu.VMEM((size_x - held, frames, size_y, size_z), signals.dtype),
            pltpu.VMEM(flags.shape, flags.dtype),
            pltpu.VMEM(basis_old.shape, basis_old.dtype),
            pltpu.SemaphoreType.DMA((size_x,)),
            pltpu.SemaphoreType.DMA((2,)),
        ],
        compiler_params=pltpu.CompilerParams(vmem_limit_bytes=limit),
        name="local_grown",
    )(signals, flags, basis_old)


def orthonormal(grown):
    rank = grown.shape[0]
    row = lax.broadcasted_iota(jnp.int32, (rank, 1), 0)
    for k in range(rank):
        pivot = grown[k : k + 1]
        inner = jnp.sum(grown * pivot, axis=1, keepdims=True)
        norm2 = inner[k : k + 1]
        scaled = pivot * (1.0 / norm2)
        grown = jnp.where(row > k, grown - inner * scaled, grown)
        grown = jnp.where(row == k, pivot / jnp.sqrt(norm2), grown)
    return grown


def project_kernel(parts, kept, signals, flags, weight, basis_out, coef, chip, gap, side, spare, sems):
    frames, count, rows, width = signals.shape
    planes = plane_refs(kept, spare)
    copies = [pltpu.make_async_copy(signals.at[:, i], planes[i], sems.at[i - held]) for i in range(held, count)]
    for copy in copies:
        copy.start()
    even = (lax.axis_index("dev") & 1) == 0
    side[...] = jnp.broadcast_to(jnp.where(even, 1, 0), side.shape)
    select = frame_select(frames, rows)
    keep = tile_masks(flags, width)
    basis = orthonormal(from_dense(jnp.sum(parts[...], axis=0)))
    rank = basis.shape[0]
    basis_out[...] = basis
    weights = mixing(basis, select, 2, rows)
    for i in range(count):
        if i >= held:
            copies[i - held].wait()
        mixed = dot(weights, rows_of(planes[i][...])).reshape(2, rows, rank, width).sum(0) * keep[i]
        coef[i] = mixed
        for y in range(2):
            chip[y * count + i] = jnp.where(even, mixed[rows - 2 + y], mixed[y])
            gap[y * count + i] = jnp.where(even, mixed[y], mixed[rows - 2 + y])
    blank = jnp.zeros((rank - count, width), jnp.float32)
    chip[2 * count, :count] = jnp.where(even, weight[:, rows - 1], weight[:, 0])
    gap[2 * count, :count] = jnp.where(even, weight[:, 0], weight[:, rows - 1])
    chip[2 * count, count:] = blank
    gap[2 * count, count:] = blank


def project(parts, kept, signals, flags, tv_weight, rank):
    frames, size_x, size_y, size_z = signals.shape
    edge = jax.ShapeDtypeStruct((2 * size_x + 1, rank, size_z), jnp.float32)
    vmem = pl.BlockSpec(memory_space=pltpu.VMEM)
    return pl.pallas_call(
        project_kernel,
        out_shape=(
            jax.ShapeDtypeStruct((rank, frames), jnp.float32),
            jax.ShapeDtypeStruct((size_x, size_y, rank, size_z), jnp.float32),
            edge,
            edge,
            jax.ShapeDtypeStruct((rank, size_z), jnp.int32),
        ),
        in_specs=[vmem, vmem, pl.BlockSpec(memory_space=pltpu.HBM), vmem, vmem],
        out_specs=(vmem,) * 5,
        scratch_shapes=[
            pltpu.VMEM((size_x - held, frames, size_y, size_z), signals.dtype),
            pltpu.SemaphoreType.DMA((size_x - held,)),
        ],
        compiler_params=pltpu.CompilerParams(vmem_limit_bytes=limit),
        name="project",
    )(parts, kept, signals, flags, tv_weight)


def slope(diff):
    return diff * lax.rsqrt(1.0 + diff * diff)


def along_z(cells):
    width = cells.shape[-1]
    lane = lax.broadcasted_iota(jnp.int32, cells.shape, cells.ndim - 1)
    above = jnp.where(lane == width - 1, 0.0, pltpu.roll(cells, width - 1, cells.ndim - 1))
    flux = slope(above - cells)
    below = jnp.where(lane == 0, slope(cells), pltpu.roll(flux, 1, cells.ndim - 1))
    return flux - below


def smooth_kernel(coef, left, right, down, up, weight, out, first, second, weights):
    count, rows, rank, width = coef.shape
    planes = count + 4
    lo, hi = slice(2, 2 + rows), slice(1, 3 + rows)
    for side, far, near in ((down, 0, 1), (up, planes - 1, planes - 2)):
        first[far, lo] = side[:rows]
        first[near, hi] = side[rows : 2 * rows + 2]
    first[2 : 2 + count, lo] = coef[...]
    for y in range(2):
        first[2 : 2 + count, y] = left[y * count : (y + 1) * count]
        first[2 : 2 + count, 2 + rows + y] = right[y * count : (y + 1) * count]
    weights[1 : 1 + count, 1 : 1 + rows] = weight[...]
    weights[1 : 1 + count, 0] = left[2 * count, :count]
    weights[1 : 1 + count, 1 + rows] = right[2 * count, :count]
    weights[0, 1 : 1 + rows] = down[2 * rows + 2]
    weights[1 + count, 1 : 1 + rows] = up[2 * rows + 2]

    def update(field, i, ys, size, before, wrow):
        cells = field[i, ys : ys + size]
        after = slope(field[i + 1, ys : ys + size] - cells)
        sides = slope(field[i, ys : ys + size + 1] - field[i, ys - 1 : ys + size])
        total = (after - before) + (sides[1:] - sides[:-1]) + along_z(cells)
        return cells + step_size * wrow[:, None, :] * total, after

    before = slope(first[1, lo] - first[0, lo])
    for i in range(1, planes - 1):
        edge = i == 1 or i == planes - 2
        ys, size = (2, rows) if edge else (1, rows + 2)
        if i == 2:
            before = slope(first[2, hi] - first[1, hi])
        if i == planes - 2:
            before = before[1 : 1 + rows]
        fresh, before = update(first, i, ys, size, before, weights[i - 1, ys - 1 : ys - 1 + size])
        second[i - 1, ys - 1 : ys - 1 + size] = fresh
    before = slope(second[1, 1 : 1 + rows] - second[0, 1 : 1 + rows])
    for i in range(1, count + 1):
        fresh, before = update(second, i, 1, rows, before, weights[i, 1 : 1 + rows])
        for y in range(rows):
            out[:, i - 1, y] = fresh[y]


def smooth(coef, left, right, down, up, tv_weight):
    count, rows, rank, width = coef.shape
    vmem = pl.BlockSpec(memory_space=pltpu.VMEM)
    return pl.pallas_call(
        smooth_kernel,
        out_shape=jax.ShapeDtypeStruct((rank, count, rows, width), jnp.float32),
        in_specs=[vmem] * 6,
        out_specs=vmem,
        scratch_shapes=[
            pltpu.VMEM((count + 4, rows + 4, rank, width), jnp.float32),
            pltpu.VMEM((count + 2, rows + 2, rank, width), jnp.float32),
            pltpu.VMEM((count + 2, rows + 2, width), jnp.float32),
        ],
        compiler_params=pltpu.CompilerParams(vmem_limit_bytes=limit),
        name="smooth",
    )(coef, left, right, down, up, tv_weight)


def neighbours(axis, toward_low, toward_high):
    ends = lax.axis_size(axis) - 1
    return (
        lax.ppermute(toward_high, axis, [(i, i + 1) for i in range(ends)]),
        lax.ppermute(toward_low, axis, [(i + 1, i) for i in range(ends)]),
    )


def neighbours_in_pairs(axis, gap, chip):
    count = lax.axis_size(axis)
    between = [(i, i + 1) for i in range(1, count - 1, 2)]
    return (
        lax.ppermute(gap, axis, between + [(j, i) for i, j in between]),
        lax.ppermute(chip, axis, [(i, i ^ 1) for i in range(count)]),
    )


def on_device(signals, tile_flags, basis_old, tv_weight):
    frames, size_x, size_y, size_z = signals.shape
    rank = basis_old.shape[1]
    flags = jnp.transpose(tile_flags, (0, 2, 1))
    pinned = [pltpu.with_memory_space_constraint(a, pltpu.HBM) for a in (signals, flags, basis_old.T)]
    parts, kept = local_grown(*pinned, lax.axis_size("grp"))
    parts = lax.all_to_all(parts, "grp", 0, 0)
    summed = jnp.sum(parts, axis=0)
    parts = jnp.broadcast_to(summed[None], (lax.axis_size("dev"),) + summed.shape)
    parts = lax.all_to_all(parts, "dev", 0, 0)
    basis, coef, chip, gap, even = project(parts, kept, pinned[0], flags, tv_weight, rank)
    gap, chip = neighbours_in_pairs("dev", gap, chip)
    left = jnp.where(even != 0, gap, chip)
    right = jnp.where(even != 0, chip, gap)

    def face(far, near):
        return jnp.concatenate(
            [coef[far], left[size_x + near][None], coef[near], right[near][None], tv_weight[near][None]], axis=0
        )

    down, up = neighbours("grp", face(1, 0), face(size_x - 2, size_x - 1))
    return (basis.T, smooth(coef, left, right, down, up, tv_weight))


def solution(mesh):
    placed = (P(None, "grp", "dev", None), P("grp", "dev", None), P(), P("grp", "dev", None))
    return jax.shard_map(
        on_device,
        mesh=mesh,
        in_specs=placed,
        out_specs=(P(), P(None, "grp", "dev", None)),
        check_vma=False,
    )
```

```python
import jax
import jax.numpy as jnp
from jax import lax
from jax.experimental import pallas as pl
from jax.experimental.pallas import tpu as pltpu
from jax.sharding import PartitionSpec as P

step_size = 0.08
limit = 44 * 1024 * 1024
ahead = 4
NT = (((1,), (1,)), ((), ()))
TN = (((0,), (0,)), ((), ()))


def dot(a, b, dims=(((1,), (0,)), ((), ()))):
    return lax.dot_general(a, b, dims, preferred_element_type=jnp.float32)


def terms(values, count):
    parts = []
    for _ in range(count):
        part = values.astype(jnp.bfloat16)
        parts.append(part)
        values = values - part.astype(jnp.float32)
    return parts


def spread_rows(repeated, rows):
    lane = lax.broadcasted_iota(jnp.int32, repeated.shape, 1) % rows
    return [jnp.where(lane == y, repeated, 0.0) for y in range(rows)]


def to_dense(values):
    rest = values[:, 128:]
    tail = jnp.concatenate([rest[:4], rest[4:]], axis=1)
    return jnp.stack([values[:4, :128], values[4:, :128], tail])


def from_dense(values):
    first = jnp.concatenate([values[0], values[1]], axis=0)
    rest = jnp.concatenate([values[2, :, :64], values[2, :, 64:]], axis=0)
    return jnp.concatenate([first, rest], axis=1)


def frame_select(frames, rows):
    shape = (frames, frames * rows)
    lane = lax.broadcasted_iota(jnp.int32, shape, 1) // rows
    return (lane == lax.broadcasted_iota(jnp.int32, shape, 0)).astype(jnp.bfloat16)


def tile_masks(flags, width):
    tiles = flags.shape[1]
    shape = (tiles, width)
    lane = lax.broadcasted_iota(jnp.int32, shape, 1) // (width // tiles)
    spread = (lane == lax.broadcasted_iota(jnp.int32, shape, 0)).astype(jnp.bfloat16)
    return [dot(flags[x].astype(jnp.bfloat16), spread, TN)[:, None, :] for x in range(flags.shape[0])]


def outer_planes(count):
    return [0, 1, count - 2, count - 1]


def inner_planes(count):
    return list(range(2, count - 2))


def rows_of(plane):
    frames, rows, width = plane.shape
    return plane.reshape(frames * rows, width)


def mixing(rows_by_frame, select, count, rows):
    spread = []
    for part in terms(rows_by_frame, count):
        spread += spread_rows(dot(part, select), rows)
    return jnp.concatenate(spread, axis=0).astype(jnp.bfloat16)


def grown_kernel(signals, flags_in, basis_in, out, kept, spare, flags, basis_old, sems, small):
    first = [
        pltpu.make_async_copy(basis_in, basis_old, small.at[0]),
        pltpu.make_async_copy(flags_in, flags, small.at[1]),
    ]
    for copy in first:
        copy.start()
    frames, count, rows, width = signals.shape
    order = outer_planes(count) + inner_planes(count)
    planes = [kept.at[i] for i in range(kept.shape[0])] + [spare.at[i] for i in range(spare.shape[0])]
    copies = [pltpu.make_async_copy(signals.at[:, x], planes[i], sems.at[i]) for i, x in enumerate(order)]
    for i in range(ahead):
        copies[i].start(priority=i % 2)
    rank = basis_old.shape[0]
    select = frame_select(frames, rows)
    for copy in first:
        copy.wait()
    weights = mixing(basis_old[...], select, 3, rows)
    keep = tile_masks(flags, width)

    def mix(i):
        flat = rows_of(planes[i][...])
        mixed = dot(weights, flat).reshape(3, rows, rank, width).sum(0) * keep[order[i]]
        return jnp.concatenate(terms(mixed.reshape(rows * rank, width), 3), axis=0), flat

    def product(mixed, flat):
        return dot(mixed, flat, NT).reshape(3, rows, rank, frames * rows).sum(0)

    total = jnp.zeros((rows, rank, frames * rows), jnp.float32)
    before = []
    for start in range(0, count, 2):
        group = range(start, start + 2)
        for i in group:
            copies[i].wait()
        for i in group:
            if i + ahead < count:
                copies[i + ahead].start(priority=(i + ahead) % 2)
        now = [mix(i) for i in group]
        for pair in before:
            total = total + product(*pair)
        before = now
    for pair in before:
        total = total + product(*pair)
    lane = lax.broadcasted_iota(jnp.int32, (rank, frames * rows), 1) % rows
    diagonal = jnp.zeros((rank, frames * rows), jnp.float32)
    for y in range(rows):
        diagonal = diagonal + jnp.where(lane == y, total[y], 0.0)
    grown = dot(jnp.concatenate(terms(diagonal, 3), axis=0), select, NT)
    grown = grown.reshape(3, rank, frames).sum(0)
    out[...] = jnp.broadcast_to(to_dense(grown)[None], out.shape)


def local_grown(signals, flags, basis_old, copies):
    frames, size_x, size_y, size_z = signals.shape
    return pl.pallas_call(
        grown_kernel,
        out_shape=(
            jax.ShapeDtypeStruct((copies, 3, 4, 128), jnp.float32),
            jax.ShapeDtypeStruct((len(outer_planes(size_x)), frames, size_y, size_z), signals.dtype),
        ),
        in_specs=[pl.BlockSpec(memory_space=pltpu.HBM)] * 3,
        out_specs=[pl.BlockSpec(memory_space=pltpu.VMEM)] * 2,
        scratch_shapes=[
            pltpu.VMEM((len(inner_planes(size_x)), frames, size_y, size_z), signals.dtype),
            pltpu.VMEM(flags.shape, flags.dtype),
            pltpu.VMEM(basis_old.shape, basis_old.dtype),
            pltpu.SemaphoreType.DMA((size_x,)),
            pltpu.SemaphoreType.DMA((2,)),
        ],
        compiler_params=pltpu.CompilerParams(vmem_limit_bytes=limit),
        name="local_grown",
    )(signals, flags, basis_old)


def orthonormal(grown):
    rank = grown.shape[0]
    row = lax.broadcasted_iota(jnp.int32, (rank, 1), 0)
    for k in range(rank):
        pivot = grown[k : k + 1]
        inner = jnp.sum(grown * pivot, axis=1, keepdims=True)
        norm2 = inner[k : k + 1]
        scaled = pivot * (1.0 / norm2)
        grown = jnp.where(row > k, grown - inner * scaled, grown)
        grown = jnp.where(row == k, pivot / jnp.sqrt(norm2), grown)
    return grown


def projected(mixer, plane, keep, rank):
    frames, rows, width = plane.shape
    return dot(mixer, rows_of(plane)).reshape(2, rows, rank, width).sum(0) * keep


def project_outer_kernel(parts, kept, flags, weight, basis_out, mixer_out, low, high, side):
    count, rows, width = weight.shape
    frames = kept.shape[1]
    even = (lax.axis_index("dev") & 1) == 0
    side[...] = jnp.broadcast_to(jnp.where(even, 1, 0), side.shape)
    select = frame_select(frames, rows)
    keep = tile_masks(flags, width)
    basis = orthonormal(from_dense(jnp.sum(parts[...], axis=0)))
    rank = basis.shape[0]
    basis_out[...] = basis
    mixer = mixing(basis, select, 2, rows)
    mixer_out[...] = mixer
    for i, x in enumerate(outer_planes(count)):
        face = low if i < 2 else high
        face[(i % 2) * rows : (i % 2 + 1) * rows] = projected(mixer, kept[i], keep[x], rank)
    low[2 * rows] = weight[0]
    high[2 * rows] = weight[count - 1]


def project_outer(parts, kept, flags, tv_weight, rank):
    size_x, size_y, size_z = tv_weight.shape
    frames = kept.shape[1]
    face = jax.ShapeDtypeStruct((2 * size_y + 1, rank, size_z), jnp.float32)
    vmem = pl.BlockSpec(memory_space=pltpu.VMEM)
    return pl.pallas_call(
        project_outer_kernel,
        out_shape=(
            jax.ShapeDtypeStruct((rank, frames), jnp.float32),
            jax.ShapeDtypeStruct((2 * size_y * rank, frames * size_y), jnp.bfloat16),
            face,
            face,
            jax.ShapeDtypeStruct((rank, size_z), jnp.int32),
        ),
        in_specs=[vmem] * 4,
        out_specs=(vmem,) * 5,
        compiler_params=pltpu.CompilerParams(vmem_limit_bytes=limit),
        name="project_outer",
    )(parts, kept, flags, tv_weight)


def project_inner_kernel(signals, mixer, flags, weight, low, high, inner, gap, planes, sems):
    frames, count, rows, width = signals.shape
    copies = [
        pltpu.make_async_copy(signals.at[:, x], planes.at[i], sems.at[i]) for i, x in enumerate(inner_planes(count))
    ]
    for copy in copies:
        copy.start()
    rank = low.shape[1]
    even = (lax.axis_index("dev") & 1) == 0
    keep = tile_masks(flags, width)

    def edges(x, head, tail):
        for y in range(2):
            gap[y * count + x] = jnp.where(even, head[y], tail[y])

    for i, x in enumerate(outer_planes(count)):
        face, first = (low if i < 2 else high), (i % 2) * rows
        edges(x, face[first : first + 2], face[first + rows - 2 : first + rows])
    blank = jnp.zeros((rank - count, width), jnp.float32)
    gap[2 * count, :count] = jnp.where(even, weight[:, 0], weight[:, rows - 1])
    gap[2 * count, count:] = blank
    for i, x in enumerate(inner_planes(count)):
        copies[i].wait()
        plane = projected(mixer[...], planes[i], keep[x], rank)
        inner[i] = plane
        edges(x, plane[:2], plane[rows - 2 :])


def project_inner(signals, mixer, flags, tv_weight, low, high):
    frames, size_x, size_y, size_z = signals.shape
    rank = low.shape[1]
    inner = len(inner_planes(size_x))
    edge = jax.ShapeDtypeStruct((2 * size_x + 1, rank, size_z), jnp.float32)
    vmem = pl.BlockSpec(memory_space=pltpu.VMEM)
    return pl.pallas_call(
        project_inner_kernel,
        out_shape=(jax.ShapeDtypeStruct((inner, size_y, rank, size_z), jnp.float32), edge),
        in_specs=[pl.BlockSpec(memory_space=pltpu.HBM)] + [vmem] * 5,
        out_specs=(vmem,) * 2,
        scratch_shapes=[
            pltpu.VMEM((inner, frames, size_y, size_z), signals.dtype),
            pltpu.SemaphoreType.DMA((inner,)),
        ],
        compiler_params=pltpu.CompilerParams(vmem_limit_bytes=limit),
        cost_estimate=pl.CostEstimate(flops=1500000000, bytes_accessed=6000000, transcendentals=0),
        name="project_inner",
    )(signals, mixer, flags, tv_weight, low, high)


def slope(diff):
    return diff * lax.rsqrt(1.0 + diff * diff)


def along_z(cells):
    width = cells.shape[-1]
    lane = lax.broadcasted_iota(jnp.int32, cells.shape, cells.ndim - 1)
    above = jnp.where(lane == width - 1, 0.0, pltpu.roll(cells, width - 1, cells.ndim - 1))
    flux = slope(above - cells)
    below = jnp.where(lane == 0, slope(cells), pltpu.roll(flux, 1, cells.ndim - 1))
    return flux - below


def update(planes, i, ys, size, before, weight):
    cells = planes[i][ys : ys + size]
    after = slope(planes[i + 1][ys : ys + size] - cells)
    sides = slope(planes[i][ys : ys + size + 1] - planes[i][ys - 1 : ys + size])
    total = (after - before) + (sides[1:] - sides[:-1]) + along_z(cells)
    return cells + step_size * weight[:, None, :] * total, after


def x_planes(low, inner, high, down, up):
    rows = inner.shape[1]
    faces = [[face.at[:rows], face.at[rows : 2 * rows]] for face in (down, low, high, up)]
    return faces[0] + faces[1] + [inner.at[i] for i in range(inner.shape[0])] + faces[2] + faces[3]


def smooth_middle_kernel(low, inner, high, down, up, weight, once, twice, chip):
    count, rows, width = weight.shape
    rank = low.shape[1]
    planes = x_planes(low, inner, high, down, up)
    even = (lax.axis_index("dev") & 1) == 0
    for x in range(count):
        for y in range(2):
            chip[y * count + x] = jnp.where(even, planes[x + 2][rows - 2 + y], planes[x + 2][y])
    chip[2 * count, :count] = jnp.where(even, weight[:, rows - 1], weight[:, 0])
    chip[2 * count, count:] = jnp.zeros((rank - count, width), jnp.float32)
    for i, plane in enumerate((planes[1], planes[count + 2])):
        chip[2 * count + 1 + i] = jnp.where(even, plane[rows - 1], plane[0])
    weights = [down.at[2 * rows]] + [weight.at[x] for x in range(count)] + [up.at[2 * rows]]
    size = rows - 2
    before = slope(planes[1][1 : 1 + size] - planes[0][1 : 1 + size])
    for i in range(1, count + 3):
        fresh, before = update(planes, i, 1, size, before, weights[i - 1][1 : 1 + size])
        once[i - 1] = fresh
    planes = [once.at[i] for i in range(count + 2)]
    size = rows - 4
    before = slope(planes[1][1 : 1 + size] - planes[0][1 : 1 + size])
    for i in range(1, count + 1):
        fresh, before = update(planes, i, 1, size, before, weight[i - 1, 2 : 2 + size])
        twice[i - 1] = fresh


def smooth_middle(low, inner, high, down, up, tv_weight):
    count, rows, width = tv_weight.shape
    rank = low.shape[1]
    vmem = pl.BlockSpec(memory_space=pltpu.VMEM)
    return pl.pallas_call(
        smooth_middle_kernel,
        out_shape=(
            jax.ShapeDtypeStruct((count + 2, rows - 2, rank, width), jnp.float32),
            jax.ShapeDtypeStruct((count, rows - 4, rank, width), jnp.float32),
            jax.ShapeDtypeStruct((2 * count + 3, rank, width), jnp.float32),
        ),
        in_specs=[vmem] * 6,
        out_specs=(vmem,) * 3,
        compiler_params=pltpu.CompilerParams(vmem_limit_bytes=limit),
        cost_estimate=pl.CostEstimate(flops=50000000, bytes_accessed=3000000, transcendentals=1000000),
        name="smooth_middle",
    )(low, inner, high, down, up, tv_weight)


def smooth_edges_kernel(low, inner, high, down, up, left, right, once, twice, weight, out, field, fresher):
    count, rows, width = weight.shape
    planes = x_planes(low, inner, high, down, up)
    last = len(planes) - 1
    for x in range(count):
        for y in range(2, rows - 2):
            out[:, x, y] = twice[x, y - 2]
    for side, received in enumerate((left, right)):
        edge = 1 if side else 2
        mine, theirs, shift = (0, 2, 2) if side else (2, 0, 0)
        outer = rows - 1 if side else 0
        own = slice(rows - 2, rows) if side else slice(0, 2)
        cells = [field.at[side, i] for i in range(last + 1)]
        for i in range(last + 1):
            cells[i][mine : mine + 2] = planes[i][own]
        for x in range(count):
            for y in range(2):
                cells[x + 2][theirs + y] = received[y * count + x]
        cells[1][3 - edge] = received[2 * count + 1]
        cells[last - 1][3 - edge] = received[2 * count + 2]
        before = slope(cells[1][edge : edge + 1] - cells[0][edge : edge + 1])
        fresh, _ = update(cells, 1, edge, 1, before, down[2 * rows, outer : outer + 1])
        fresher[side, 0, shift + edge - 1] = fresh[0]
        before = slope(cells[2][1:3] - cells[1][1:3])
        for x in range(count):
            pair = [weight[x, outer : outer + 1], received[2 * count, x : x + 1]]
            pair = jnp.concatenate(pair if side else pair[::-1], axis=0)
            fresh, before = update(cells, x + 2, 1, 2, before, pair)
            fresher[side, x + 1, shift : shift + 2] = fresh
        before = before[edge - 1 : edge]
        fresh, _ = update(cells, last - 1, edge, 1, before, up[2 * rows, outer : outer + 1])
        fresher[side, count + 1, shift + edge - 1] = fresh[0]
        done = slice(rows - 4, rows - 2) if side else slice(0, 2)
        cells = [fresher.at[side, i] for i in range(count + 2)]
        for i in range(count + 2):
            cells[i][2 - shift : 4 - shift] = once[i, done]
        before = slope(cells[1][1:3] - cells[0][1:3])
        for x in range(count):
            fresh, before = update(cells, x + 1, 1, 2, before, weight[x, own])
            for y in range(2):
                out[:, x, own.start + y] = fresh[y]


def smooth_edges(low, inner, high, down, up, left, right, once, twice, tv_weight):
    count, rows, width = tv_weight.shape
    rank = low.shape[1]
    vmem = pl.BlockSpec(memory_space=pltpu.VMEM)
    return pl.pallas_call(
        smooth_edges_kernel,
        out_shape=jax.ShapeDtypeStruct((rank, count, rows, width), jnp.float32),
        in_specs=[vmem] * 10,
        out_specs=vmem,
        scratch_shapes=[
            pltpu.VMEM((2, count + 4, 4, rank, width), jnp.float32),
            pltpu.VMEM((2, count + 2, 4, rank, width), jnp.float32),
        ],
        compiler_params=pltpu.CompilerParams(vmem_limit_bytes=limit),
        name="smooth_edges",
    )(low, inner, high, down, up, left, right, once, twice, tv_weight)


def neighbours(axis, toward_low, toward_high):
    ends = lax.axis_size(axis) - 1
    return (
        lax.ppermute(toward_high, axis, [(i, i + 1) for i in range(ends)]),
        lax.ppermute(toward_low, axis, [(i + 1, i) for i in range(ends)]),
    )


def neighbours_in_pairs(axis, gap, chip):
    count = lax.axis_size(axis)
    between = [(i, i + 1) for i in range(1, count - 1, 2)]
    return (
        lax.ppermute(gap, axis, between + [(j, i) for i, j in between]),
        lax.ppermute(chip, axis, [(i, i ^ 1) for i in range(count)]),
    )


def on_device(signals, tile_flags, basis_old, tv_weight):
    frames, size_x, size_y, size_z = signals.shape
    rank = basis_old.shape[1]
    flags = jnp.transpose(tile_flags, (0, 2, 1))
    pinned = [pltpu.with_memory_space_constraint(a, pltpu.HBM) for a in (signals, flags, basis_old.T)]
    parts, kept = local_grown(*pinned, lax.axis_size("grp"))
    parts = lax.all_to_all(parts, "grp", 0, 0)
    summed = jnp.sum(parts, axis=0)
    parts = jnp.broadcast_to(summed[None], (lax.axis_size("dev"),) + summed.shape)
    parts = lax.all_to_all(parts, "dev", 0, 0)
    basis, mixer, low, high, even = project_outer(parts, kept, flags, tv_weight, rank)
    down, up = neighbours("grp", low, high)
    inner, gap = project_inner(pinned[0], mixer, flags, tv_weight, low, high)
    heads = jnp.stack([down[size_y], up[0]])
    tails = jnp.stack([down[2 * size_y - 1], up[size_y - 1]])
    gap = jnp.concatenate([gap, jnp.where(even != 0, heads, tails)], axis=0)
    once, twice, chip = smooth_middle(low, inner, high, down, up, tv_weight)
    gap, chip = neighbours_in_pairs("dev", gap, chip)
    left = jnp.where(even != 0, gap, chip)
    right = jnp.where(even != 0, chip, gap)
    return (basis.T, smooth_edges(low, inner, high, down, up, left, right, once, twice, tv_weight))


def solution(mesh):
    placed = (P(None, "grp", "dev", None), P("grp", "dev", None), P(), P("grp", "dev", None))
    return jax.shard_map(
        on_device,
        mesh=mesh,
        in_specs=placed,
        out_specs=(P(), P(None, "grp", "dev", None)),
        check_vma=False,
    )
```

```python
import jax
import jax.numpy as jnp
from jax import lax
from jax.experimental import pallas as pl
from jax.experimental.pallas import tpu as pltpu
from jax.sharding import PartitionSpec as P

step_size = 0.08
limit = 44 * 1024 * 1024
ahead = 4
NT = (((1,), (1,)), ((), ()))
TN = (((0,), (0,)), ((), ()))


def dot(a, b, dims=(((1,), (0,)), ((), ()))):
    return lax.dot_general(a, b, dims, preferred_element_type=jnp.float32)


def terms(values, count):
    parts = []
    for _ in range(count):
        part = values.astype(jnp.bfloat16)
        parts.append(part)
        values = values - part.astype(jnp.float32)
    return parts


def spread_rows(repeated, rows):
    lane = lax.broadcasted_iota(jnp.int32, repeated.shape, 1) % rows
    return [jnp.where(lane == y, repeated, 0.0) for y in range(rows)]


def to_dense(values):
    rest = values[:, 128:]
    tail = jnp.concatenate([rest[:4], rest[4:]], axis=1)
    return jnp.stack([values[:4, :128], values[4:, :128], tail])


def from_dense(values):
    first = jnp.concatenate([values[0], values[1]], axis=0)
    rest = jnp.concatenate([values[2, :, :64], values[2, :, 64:]], axis=0)
    return jnp.concatenate([first, rest], axis=1)


def frame_select(frames, rows):
    shape = (frames, frames * rows)
    lane = lax.broadcasted_iota(jnp.int32, shape, 1) // rows
    return (lane == lax.broadcasted_iota(jnp.int32, shape, 0)).astype(jnp.bfloat16)


def tile_masks(flags, width):
    tiles = flags.shape[1]
    shape = (tiles, width)
    lane = lax.broadcasted_iota(jnp.int32, shape, 1) // (width // tiles)
    spread = (lane == lax.broadcasted_iota(jnp.int32, shape, 0)).astype(jnp.bfloat16)
    return [dot(flags[x].astype(jnp.bfloat16), spread, TN)[:, None, :] for x in range(flags.shape[0])]


def outer_planes(count):
    return [0, 1, count - 2, count - 1]


def inner_planes(count):
    return list(range(2, count - 2))


def rows_of(plane):
    frames, rows, width = plane.shape
    return plane.reshape(frames * rows, width)


def mixing(rows_by_frame, select, count, rows):
    spread = []
    for part in terms(rows_by_frame, count):
        spread += spread_rows(dot(part, select), rows)
    return jnp.concatenate(spread, axis=0).astype(jnp.bfloat16)


def grown_kernel(signals, flags_in, basis_in, out, kept, spare, flags, basis_old, sems, small):
    first = [
        pltpu.make_async_copy(basis_in, basis_old, small.at[0]),
        pltpu.make_async_copy(flags_in, flags, small.at[1]),
    ]
    for copy in first:
        copy.start()
    frames, count, rows, width = signals.shape
    order = outer_planes(count) + inner_planes(count)
    planes = [kept.at[i] for i in range(kept.shape[0])] + [spare.at[i] for i in range(spare.shape[0])]
    copies = [pltpu.make_async_copy(signals.at[:, x], planes[i], sems.at[i]) for i, x in enumerate(order)]
    for i in range(ahead):
        copies[i].start(priority=i % 2)
    rank = basis_old.shape[0]
    select = frame_select(frames, rows)
    for copy in first:
        copy.wait()
    weights = mixing(basis_old[...], select, 3, rows)
    keep = tile_masks(flags, width)

    def mix(i):
        flat = rows_of(planes[i][...])
        mixed = dot(weights, flat).reshape(3, rows, rank, width).sum(0) * keep[order[i]]
        return jnp.concatenate(terms(mixed.reshape(rows * rank, width), 3), axis=0), flat

    def product(mixed, flat):
        return dot(mixed, flat, NT).reshape(3, rows, rank, frames * rows).sum(0)

    total = jnp.zeros((rows, rank, frames * rows), jnp.float32)
    before = []
    for start in range(0, count, 2):
        group = range(start, start + 2)
        for i in group:
            copies[i].wait()
        for i in group:
            if i + ahead < count:
                copies[i + ahead].start(priority=(i + ahead) % 2)
        now = [mix(i) for i in group]
        for pair in before:
            total = total + product(*pair)
        before = now
    for pair in before:
        total = total + product(*pair)
    lane = lax.broadcasted_iota(jnp.int32, (rank, frames * rows), 1) % rows
    diagonal = jnp.zeros((rank, frames * rows), jnp.float32)
    for y in range(rows):
        diagonal = diagonal + jnp.where(lane == y, total[y], 0.0)
    grown = dot(jnp.concatenate(terms(diagonal, 3), axis=0), select, NT)
    grown = grown.reshape(3, rank, frames).sum(0)
    out[...] = jnp.broadcast_to(to_dense(grown)[None], out.shape)


def local_grown(signals, flags, basis_old, copies):
    frames, size_x, size_y, size_z = signals.shape
    return pl.pallas_call(
        grown_kernel,
        out_shape=(
            jax.ShapeDtypeStruct((copies, 3, 4, 128), jnp.float32),
            jax.ShapeDtypeStruct((len(outer_planes(size_x)), frames, size_y, size_z), signals.dtype),
        ),
        in_specs=[pl.BlockSpec(memory_space=pltpu.HBM)] * 3,
        out_specs=[pl.BlockSpec(memory_space=pltpu.VMEM)] * 2,
        scratch_shapes=[
            pltpu.VMEM((len(inner_planes(size_x)), frames, size_y, size_z), signals.dtype),
            pltpu.VMEM(flags.shape, flags.dtype),
            pltpu.VMEM(basis_old.shape, basis_old.dtype),
            pltpu.SemaphoreType.DMA((size_x,)),
            pltpu.SemaphoreType.DMA((2,)),
        ],
        compiler_params=pltpu.CompilerParams(vmem_limit_bytes=limit),
        name="local_grown",
    )(signals, flags, basis_old)


def orthonormal(grown):
    rank = grown.shape[0]
    row = lax.broadcasted_iota(jnp.int32, (rank, 1), 0)
    for k in range(rank):
        pivot = grown[k : k + 1]
        inner = jnp.sum(grown * pivot, axis=1, keepdims=True)
        norm2 = inner[k : k + 1]
        grown = jnp.where(row > k, grown - (inner / norm2) * pivot, grown)
        grown = jnp.where(row == k, pivot / jnp.sqrt(norm2), grown)
    return grown


def projected(mixer, plane, keep, rank):
    frames, rows, width = plane.shape
    return dot(mixer, rows_of(plane)).reshape(2, rows, rank, width).sum(0) * keep


def project_outer_kernel(parts, kept, flags, weight, basis_out, mixer_out, low, high, side):
    count, rows, width = weight.shape
    frames = kept.shape[1]
    even = (lax.axis_index("dev") & 1) == 0
    side[...] = jnp.broadcast_to(jnp.where(even, 1, 0), side.shape)
    select = frame_select(frames, rows)
    keep = tile_masks(flags, width)
    basis = orthonormal(from_dense(jnp.sum(parts[...], axis=0)))
    rank = basis.shape[0]
    basis_out[...] = basis
    mixer = mixing(basis, select, 2, rows)
    mixer_out[...] = mixer
    for i, x in enumerate(outer_planes(count)):
        face = low if i < 2 else high
        face[(i % 2) * rows : (i % 2 + 1) * rows] = projected(mixer, kept[i], keep[x], rank)
    low[2 * rows] = weight[0]
    high[2 * rows] = weight[count - 1]


def project_outer(parts, kept, flags, tv_weight, rank):
    size_x, size_y, size_z = tv_weight.shape
    frames = kept.shape[1]
    face = jax.ShapeDtypeStruct((2 * size_y + 1, rank, size_z), jnp.float32)
    vmem = pl.BlockSpec(memory_space=pltpu.VMEM)
    return pl.pallas_call(
        project_outer_kernel,
        out_shape=(
            jax.ShapeDtypeStruct((rank, frames), jnp.float32),
            jax.ShapeDtypeStruct((2 * size_y * rank, frames * size_y), jnp.bfloat16),
            face,
            face,
            jax.ShapeDtypeStruct((rank, size_z), jnp.int32),
        ),
        in_specs=[vmem] * 4,
        out_specs=(vmem,) * 5,
        compiler_params=pltpu.CompilerParams(vmem_limit_bytes=limit),
        name="project_outer",
    )(parts, kept, flags, tv_weight)


def project_inner_kernel(signals, mixer, flags, weight, low, high, inner, chip, gap, planes, sems):
    frames, count, rows, width = signals.shape
    copies = [
        pltpu.make_async_copy(signals.at[:, x], planes.at[i], sems.at[i]) for i, x in enumerate(inner_planes(count))
    ]
    for copy in copies:
        copy.start()
    rank = low.shape[1]
    even = (lax.axis_index("dev") & 1) == 0
    keep = tile_masks(flags, width)

    def edges(x, head, tail):
        for y in range(2):
            chip[y * count + x] = jnp.where(even, tail[y], head[y])
            gap[y * count + x] = jnp.where(even, head[y], tail[y])

    for i, x in enumerate(outer_planes(count)):
        face, first = (low if i < 2 else high), (i % 2) * rows
        edges(x, face[first : first + 2], face[first + rows - 2 : first + rows])
    blank = jnp.zeros((rank - count, width), jnp.float32)
    chip[2 * count, :count] = jnp.where(even, weight[:, rows - 1], weight[:, 0])
    gap[2 * count, :count] = jnp.where(even, weight[:, 0], weight[:, rows - 1])
    chip[2 * count, count:] = blank
    gap[2 * count, count:] = blank
    for i, x in enumerate(inner_planes(count)):
        copies[i].wait()
        plane = projected(mixer[...], planes[i], keep[x], rank)
        inner[i] = plane
        edges(x, plane[:2], plane[rows - 2 :])


def project_inner(signals, mixer, flags, tv_weight, low, high):
    frames, size_x, size_y, size_z = signals.shape
    rank = low.shape[1]
    inner = len(inner_planes(size_x))
    edge = jax.ShapeDtypeStruct((2 * size_x + 1, rank, size_z), jnp.float32)
    vmem = pl.BlockSpec(memory_space=pltpu.VMEM)
    return pl.pallas_call(
        project_inner_kernel,
        out_shape=(jax.ShapeDtypeStruct((inner, size_y, rank, size_z), jnp.float32), edge, edge),
        in_specs=[pl.BlockSpec(memory_space=pltpu.HBM)] + [vmem] * 5,
        out_specs=(vmem,) * 3,
        scratch_shapes=[
            pltpu.VMEM((inner, frames, size_y, size_z), signals.dtype),
            pltpu.SemaphoreType.DMA((inner,)),
        ],
        compiler_params=pltpu.CompilerParams(vmem_limit_bytes=limit),
        cost_estimate=pl.CostEstimate(flops=1500000000, bytes_accessed=6000000, transcendentals=0),
        name="project_inner",
    )(signals, mixer, flags, tv_weight, low, high)


def slope(diff):
    return diff * lax.rsqrt(1.0 + diff * diff)


def along_z(cells):
    width = cells.shape[-1]
    lane = lax.broadcasted_iota(jnp.int32, cells.shape, cells.ndim - 1)
    above = jnp.where(lane == width - 1, 0.0, pltpu.roll(cells, width - 1, cells.ndim - 1))
    flux = slope(above - cells)
    below = jnp.where(lane == 0, slope(cells), pltpu.roll(flux, 1, cells.ndim - 1))
    return flux - below


def update(planes, i, ys, size, before, weight):
    cells = planes[i][ys : ys + size]
    after = slope(planes[i + 1][ys : ys + size] - cells)
    sides = slope(planes[i][ys : ys + size + 1] - planes[i][ys - 1 : ys + size])
    total = (after - before) + (sides[1:] - sides[:-1]) + along_z(cells)
    return cells + step_size * weight[:, None, :] * total, after


def x_planes(low, inner, high, down, up):
    rows = inner.shape[1]
    faces = [[face.at[:rows], face.at[rows : 2 * rows]] for face in (down, low, high, up)]
    return faces[0] + faces[1] + [inner.at[i] for i in range(inner.shape[0])] + faces[2] + faces[3]


def smooth_middle_kernel(low, inner, high, down, up, weight, once, twice):
    count, rows, width = weight.shape
    planes = x_planes(low, inner, high, down, up)
    weights = [down.at[2 * rows]] + [weight.at[x] for x in range(count)] + [up.at[2 * rows]]
    size = rows - 2
    before = slope(planes[1][1 : 1 + size] - planes[0][1 : 1 + size])
    for i in range(1, count + 3):
        fresh, before = update(planes, i, 1, size, before, weights[i - 1][1 : 1 + size])
        once[i - 1] = fresh
    planes = [once.at[i] for i in range(count + 2)]
    size = rows - 4
    before = slope(planes[1][1 : 1 + size] - planes[0][1 : 1 + size])
    for i in range(1, count + 1):
        fresh, before = update(planes, i, 1, size, before, weight[i - 1, 2 : 2 + size])
        twice[i - 1] = fresh


def smooth_middle(low, inner, high, down, up, tv_weight):
    count, rows, width = tv_weight.shape
    rank = low.shape[1]
    vmem = pl.BlockSpec(memory_space=pltpu.VMEM)
    return pl.pallas_call(
        smooth_middle_kernel,
        out_shape=(
            jax.ShapeDtypeStruct((count + 2, rows - 2, rank, width), jnp.float32),
            jax.ShapeDtypeStruct((count, rows - 4, rank, width), jnp.float32),
        ),
        in_specs=[vmem] * 6,
        out_specs=(vmem,) * 2,
        compiler_params=pltpu.CompilerParams(vmem_limit_bytes=limit),
        cost_estimate=pl.CostEstimate(flops=50000000, bytes_accessed=3000000, transcendentals=1000000),
        name="smooth_middle",
    )(low, inner, high, down, up, tv_weight)


def smooth_edges_kernel(low, inner, high, down, up, left, right, once, twice, weight, out, field, fresher):
    count, rows, width = weight.shape
    planes = x_planes(low, inner, high, down, up)
    last = len(planes) - 1
    for x in range(count):
        for y in range(2, rows - 2):
            out[:, x, y] = twice[x, y - 2]
    for side, received in enumerate((left, right)):
        edge = 1 if side else 2
        mine, theirs, shift = (0, 2, 2) if side else (2, 0, 0)
        outer = rows - 1 if side else 0
        own = slice(rows - 2, rows) if side else slice(0, 2)
        cells = [field.at[side, i] for i in range(last + 1)]
        for i in range(last + 1):
            cells[i][mine : mine + 2] = planes[i][own]
        for x in range(count):
            for y in range(2):
                cells[x + 2][theirs + y] = received[y * count + x]
        cells[1][3 - edge] = received[2 * count + 1]
        cells[last - 1][3 - edge] = received[2 * count + 2]
        before = slope(cells[1][edge : edge + 1] - cells[0][edge : edge + 1])
        fresh, _ = update(cells, 1, edge, 1, before, down[2 * rows, outer : outer + 1])
        fresher[side, 0, shift + edge - 1] = fresh[0]
        before = slope(cells[2][1:3] - cells[1][1:3])
        for x in range(count):
            pair = [weight[x, outer : outer + 1], received[2 * count, x : x + 1]]
            pair = jnp.concatenate(pair if side else pair[::-1], axis=0)
            fresh, before = update(cells, x + 2, 1, 2, before, pair)
            fresher[side, x + 1, shift : shift + 2] = fresh
        before = before[edge - 1 : edge]
        fresh, _ = update(cells, last - 1, edge, 1, before, up[2 * rows, outer : outer + 1])
        fresher[side, count + 1, shift + edge - 1] = fresh[0]
        done = slice(rows - 4, rows - 2) if side else slice(0, 2)
        cells = [fresher.at[side, i] for i in range(count + 2)]
        for i in range(count + 2):
            cells[i][2 - shift : 4 - shift] = once[i, done]
        before = slope(cells[1][1:3] - cells[0][1:3])
        for x in range(count):
            fresh, before = update(cells, x + 1, 1, 2, before, weight[x, own])
            for y in range(2):
                out[:, x, own.start + y] = fresh[y]


def smooth_edges(low, inner, high, down, up, left, right, once, twice, tv_weight):
    count, rows, width = tv_weight.shape
    rank = low.shape[1]
    vmem = pl.BlockSpec(memory_space=pltpu.VMEM)
    return pl.pallas_call(
        smooth_edges_kernel,
        out_shape=jax.ShapeDtypeStruct((rank, count, rows, width), jnp.float32),
        in_specs=[vmem] * 10,
        out_specs=vmem,
        scratch_shapes=[
            pltpu.VMEM((2, count + 4, 4, rank, width), jnp.float32),
            pltpu.VMEM((2, count + 2, 4, rank, width), jnp.float32),
        ],
        compiler_params=pltpu.CompilerParams(vmem_limit_bytes=limit),
        name="smooth_edges",
    )(low, inner, high, down, up, left, right, once, twice, tv_weight)


def neighbours(axis, toward_low, toward_high):
    ends = lax.axis_size(axis) - 1
    return (
        lax.ppermute(toward_high, axis, [(i, i + 1) for i in range(ends)]),
        lax.ppermute(toward_low, axis, [(i + 1, i) for i in range(ends)]),
    )


def neighbours_in_pairs(axis, gap, chip):
    count = lax.axis_size(axis)
    between = [(i, i + 1) for i in range(1, count - 1, 2)]
    return (
        lax.ppermute(gap, axis, between + [(j, i) for i, j in between]),
        lax.ppermute(chip, axis, [(i, i ^ 1) for i in range(count)]),
    )


def on_device(signals, tile_flags, basis_old, tv_weight):
    frames, size_x, size_y, size_z = signals.shape
    rank = basis_old.shape[1]
    flags = jnp.transpose(tile_flags, (0, 2, 1))
    pinned = [pltpu.with_memory_space_constraint(a, pltpu.HBM) for a in (signals, flags, basis_old.T)]
    parts, kept = local_grown(*pinned, lax.axis_size("dev"))
    parts = lax.all_to_all(parts, "dev", 0, 0)
    summed = jnp.sum(parts, axis=0)
    parts = jnp.broadcast_to(summed[None], (lax.axis_size("grp"),) + summed.shape)
    parts = lax.all_to_all(parts, "grp", 0, 0)
    basis, mixer, low, high, even = project_outer(parts, kept, flags, tv_weight, rank)
    down, up = neighbours("grp", low, high)
    inner, chip, gap = project_inner(pinned[0], mixer, flags, tv_weight, low, high)
    heads = jnp.stack([down[size_y], up[0]])
    tails = jnp.stack([down[2 * size_y - 1], up[size_y - 1]])
    chip = jnp.concatenate([chip, jnp.where(even != 0, tails, heads)], axis=0)
    gap = jnp.concatenate([gap, jnp.where(even != 0, heads, tails)], axis=0)
    gap, chip = neighbours_in_pairs("dev", gap, chip)
    once, twice = smooth_middle(low, inner, high, down, up, tv_weight)
    left = jnp.where(even == 0, chip, gap)
    right = jnp.where(even == 0, gap, chip)
    return (basis.T, smooth_edges(low, inner, high, down, up, left, right, once, twice, tv_weight))


def solution(mesh):
    placed = (P(None, "grp", "dev", None), P("grp", "dev", None), P(), P("grp", "dev", None))
    return jax.shard_map(
        on_device,
        mesh=mesh,
        in_specs=placed,
        out_specs=(P(), P(None, "grp", "dev", None)),
        check_vma=False,
    )
```

```python
import jax
import jax.numpy as jnp
from jax import lax
from jax.experimental import pallas as pl
from jax.experimental.pallas import tpu as pltpu
from jax.sharding import PartitionSpec as P

step_size = 0.08
limit = 44 * 1024 * 1024
ahead = 4
NT = (((1,), (1,)), ((), ()))
TN = (((0,), (0,)), ((), ()))


def dot(a, b, dims=(((1,), (0,)), ((), ()))):
    return lax.dot_general(a, b, dims, preferred_element_type=jnp.float32)


def terms(values, count):
    parts = []
    for _ in range(count):
        part = values.astype(jnp.bfloat16)
        parts.append(part)
        values = values - part.astype(jnp.float32)
    return parts


def spread_rows(repeated, rows):
    lane = lax.broadcasted_iota(jnp.int32, repeated.shape, 1) % rows
    return [jnp.where(lane == y, repeated, 0.0) for y in range(rows)]


def to_dense(values):
    rest = values[:, 128:]
    tail = jnp.concatenate([rest[:4], rest[4:]], axis=1)
    return jnp.stack([values[:4, :128], values[4:, :128], tail])


def from_dense(values):
    first = jnp.concatenate([values[0], values[1]], axis=0)
    rest = jnp.concatenate([values[2, :, :64], values[2, :, 64:]], axis=0)
    return jnp.concatenate([first, rest], axis=1)


def frame_select(frames, rows):
    shape = (frames, frames * rows)
    lane = lax.broadcasted_iota(jnp.int32, shape, 1) // rows
    return (lane == lax.broadcasted_iota(jnp.int32, shape, 0)).astype(jnp.bfloat16)


def tile_masks(flags, width):
    tiles = flags.shape[1]
    shape = (tiles, width)
    lane = lax.broadcasted_iota(jnp.int32, shape, 1) // (width // tiles)
    spread = (lane == lax.broadcasted_iota(jnp.int32, shape, 0)).astype(jnp.bfloat16)
    return [dot(flags[x].astype(jnp.bfloat16), spread, TN)[:, None, :] for x in range(flags.shape[0])]


def outer_planes(count):
    return [0, 1, count - 2, count - 1]


def inner_planes(count):
    return list(range(2, count - 2))


def rows_of(plane):
    frames, rows, width = plane.shape
    return plane.reshape(frames * rows, width)


def mixing(rows_by_frame, select, count, rows):
    spread = []
    for part in terms(rows_by_frame, count):
        spread += spread_rows(dot(part, select), rows)
    return jnp.concatenate(spread, axis=0).astype(jnp.bfloat16)


def grown_kernel(signals, flags_in, basis_in, out, kept, spare, flags, basis_old, sems, small):
    first = [
        pltpu.make_async_copy(basis_in, basis_old, small.at[0]),
        pltpu.make_async_copy(flags_in, flags, small.at[1]),
    ]
    for copy in first:
        copy.start()
    frames, count, rows, width = signals.shape
    order = outer_planes(count) + inner_planes(count)
    planes = [kept.at[i] for i in range(kept.shape[0])] + [spare.at[i] for i in range(spare.shape[0])]
    copies = [pltpu.make_async_copy(signals.at[:, x], planes[i], sems.at[i]) for i, x in enumerate(order)]
    for i in range(ahead):
        copies[i].start(priority=i % 2)
    rank = basis_old.shape[0]
    select = frame_select(frames, rows)
    for copy in first:
        copy.wait()
    weights = mixing(basis_old[...], select, 3, rows)
    keep = tile_masks(flags, width)

    def mix(i):
        flat = rows_of(planes[i][...])
        mixed = dot(weights, flat).reshape(3, rows, rank, width).sum(0) * keep[order[i]]
        return jnp.concatenate(terms(mixed.reshape(rows * rank, width), 3), axis=0), flat

    def product(mixed, flat):
        return dot(mixed, flat, NT).reshape(3, rows, rank, frames * rows).sum(0)

    total = jnp.zeros((rows, rank, frames * rows), jnp.float32)
    before = []
    for start in range(0, count, 2):
        group = range(start, start + 2)
        for i in group:
            copies[i].wait()
        for i in group:
            if i + ahead < count:
                copies[i + ahead].start(priority=(i + ahead) % 2)
        now = [mix(i) for i in group]
        for pair in before:
            total = total + product(*pair)
        before = now
    for pair in before:
        total = total + product(*pair)
    lane = lax.broadcasted_iota(jnp.int32, (rank, frames * rows), 1) % rows
    diagonal = jnp.zeros((rank, frames * rows), jnp.float32)
    for y in range(rows):
        diagonal = diagonal + jnp.where(lane == y, total[y], 0.0)
    grown = dot(jnp.concatenate(terms(diagonal, 3), axis=0), select, NT)
    grown = grown.reshape(3, rank, frames).sum(0)
    out[...] = jnp.broadcast_to(to_dense(grown)[None], out.shape)


def local_grown(signals, flags, basis_old, copies):
    frames, size_x, size_y, size_z = signals.shape
    return pl.pallas_call(
        grown_kernel,
        out_shape=(
            jax.ShapeDtypeStruct((copies, 3, 4, 128), jnp.float32),
            jax.ShapeDtypeStruct((len(outer_planes(size_x)), frames, size_y, size_z), signals.dtype),
        ),
        in_specs=[pl.BlockSpec(memory_space=pltpu.HBM)] * 3,
        out_specs=[pl.BlockSpec(memory_space=pltpu.VMEM)] * 2,
        scratch_shapes=[
            pltpu.VMEM((len(inner_planes(size_x)), frames, size_y, size_z), signals.dtype),
            pltpu.VMEM(flags.shape, flags.dtype),
            pltpu.VMEM(basis_old.shape, basis_old.dtype),
            pltpu.SemaphoreType.DMA((size_x,)),
            pltpu.SemaphoreType.DMA((2,)),
        ],
        compiler_params=pltpu.CompilerParams(vmem_limit_bytes=limit),
        name="local_grown",
    )(signals, flags, basis_old)


def orthonormal(grown):
    rank = grown.shape[0]
    row = lax.broadcasted_iota(jnp.int32, (rank, 1), 0)
    for k in range(rank):
        pivot = grown[k : k + 1]
        inner = jnp.sum(grown * pivot, axis=1, keepdims=True)
        norm2 = inner[k : k + 1]
        grown = jnp.where(row > k, grown - (inner / norm2) * pivot, grown)
        grown = jnp.where(row == k, pivot / jnp.sqrt(norm2), grown)
    return grown


def projected(mixer, plane, keep, rank):
    frames, rows, width = plane.shape
    return dot(mixer, rows_of(plane)).reshape(2, rows, rank, width).sum(0) * keep


def project_outer_kernel(parts, kept, flags, weight, basis_out, mixer_out, low, high, side):
    count, rows, width = weight.shape
    frames = kept.shape[1]
    even = (lax.axis_index("dev") & 1) == 0
    side[...] = jnp.broadcast_to(jnp.where(even, 1, 0), side.shape)
    select = frame_select(frames, rows)
    keep = tile_masks(flags, width)
    basis = orthonormal(from_dense(jnp.sum(parts[...], axis=0)))
    rank = basis.shape[0]
    basis_out[...] = basis
    mixer = mixing(basis, select, 2, rows)
    mixer_out[...] = mixer
    for i, x in enumerate(outer_planes(count)):
        face = low if i < 2 else high
        face[(i % 2) * rows : (i % 2 + 1) * rows] = projected(mixer, kept[i], keep[x], rank)
    low[2 * rows] = weight[0]
    high[2 * rows] = weight[count - 1]


def project_outer(parts, kept, flags, tv_weight, rank):
    size_x, size_y, size_z = tv_weight.shape
    frames = kept.shape[1]
    face = jax.ShapeDtypeStruct((2 * size_y + 1, rank, size_z), jnp.float32)
    vmem = pl.BlockSpec(memory_space=pltpu.VMEM)
    return pl.pallas_call(
        project_outer_kernel,
        out_shape=(
            jax.ShapeDtypeStruct((rank, frames), jnp.float32),
            jax.ShapeDtypeStruct((2 * size_y * rank, frames * size_y), jnp.bfloat16),
            face,
            face,
            jax.ShapeDtypeStruct((rank, size_z), jnp.int32),
        ),
        in_specs=[vmem] * 4,
        out_specs=(vmem,) * 5,
        compiler_params=pltpu.CompilerParams(vmem_limit_bytes=limit),
        name="project_outer",
    )(parts, kept, flags, tv_weight)


def project_inner_kernel(signals, mixer, flags, weight, low, high, inner, chip, gap, planes, sems):
    frames, count, rows, width = signals.shape
    copies = [
        pltpu.make_async_copy(signals.at[:, x], planes.at[i], sems.at[i]) for i, x in enumerate(inner_planes(count))
    ]
    for copy in copies:
        copy.start()
    rank = low.shape[1]
    even = (lax.axis_index("dev") & 1) == 0
    keep = tile_masks(flags, width)

    def edges(x, head, tail):
        for y in range(2):
            chip[y * count + x] = jnp.where(even, tail[y], head[y])
            gap[y * count + x] = jnp.where(even, head[y], tail[y])

    for i, x in enumerate(outer_planes(count)):
        face, first = (low if i < 2 else high), (i % 2) * rows
        edges(x, face[first : first + 2], face[first + rows - 2 : first + rows])
    blank = jnp.zeros((rank - count, width), jnp.float32)
    chip[2 * count, :count] = jnp.where(even, weight[:, rows - 1], weight[:, 0])
    gap[2 * count, :count] = jnp.where(even, weight[:, 0], weight[:, rows - 1])
    chip[2 * count, count:] = blank
    gap[2 * count, count:] = blank
    for i, x in enumerate(inner_planes(count)):
        copies[i].wait()
        plane = projected(mixer[...], planes[i], keep[x], rank)
        inner[i] = plane
        edges(x, plane[:2], plane[rows - 2 :])


def project_inner(signals, mixer, flags, tv_weight, low, high):
    frames, size_x, size_y, size_z = signals.shape
    rank = low.shape[1]
    inner = len(inner_planes(size_x))
    edge = jax.ShapeDtypeStruct((2 * size_x + 1, rank, size_z), jnp.float32)
    vmem = pl.BlockSpec(memory_space=pltpu.VMEM)
    return pl.pallas_call(
        project_inner_kernel,
        out_shape=(jax.ShapeDtypeStruct((inner, size_y, rank, size_z), jnp.float32), edge, edge),
        in_specs=[pl.BlockSpec(memory_space=pltpu.HBM)] + [vmem] * 5,
        out_specs=(vmem,) * 3,
        scratch_shapes=[
            pltpu.VMEM((inner, frames, size_y, size_z), signals.dtype),
            pltpu.SemaphoreType.DMA((inner,)),
        ],
        compiler_params=pltpu.CompilerParams(vmem_limit_bytes=limit),
        cost_estimate=pl.CostEstimate(flops=1500000000, bytes_accessed=6000000, transcendentals=0),
        name="project_inner",
    )(signals, mixer, flags, tv_weight, low, high)


def slope(diff):
    return diff * lax.rsqrt(1.0 + diff * diff)


def along_z(cells):
    width = cells.shape[-1]
    lane = lax.broadcasted_iota(jnp.int32, cells.shape, cells.ndim - 1)
    above = jnp.where(lane == width - 1, 0.0, pltpu.roll(cells, width - 1, cells.ndim - 1))
    flux = slope(above - cells)
    below = jnp.where(lane == 0, slope(cells), pltpu.roll(flux, 1, cells.ndim - 1))
    return flux - below


def update(planes, i, ys, size, before, weight):
    cells = planes[i][ys : ys + size]
    after = slope(planes[i + 1][ys : ys + size] - cells)
    sides = slope(planes[i][ys : ys + size + 1] - planes[i][ys - 1 : ys + size])
    total = (after - before) + (sides[1:] - sides[:-1]) + along_z(cells)
    return cells + step_size * weight[:, None, :] * total, after


def update_planes(field, first, count, weight):
    stop = first + count
    cells = field[first:stop, 1:3]
    along_x = slope(field[first : stop + 1, 1:3] - field[first - 1 : stop, 1:3])
    along_y = slope(field[first:stop, 1:4] - field[first:stop, 0:3])
    total = (along_x[1:] - along_x[:-1]) + (along_y[:, 1:] - along_y[:, :-1]) + along_z(cells)
    return cells + step_size * weight[:, :, None, :] * total


def x_planes(low, inner, high, down, up):
    rows = inner.shape[1]
    faces = [[face.at[:rows], face.at[rows : 2 * rows]] for face in (down, low, high, up)]
    return faces[0] + faces[1] + [inner.at[i] for i in range(inner.shape[0])] + faces[2] + faces[3]


def smooth_middle_kernel(low, inner, high, down, up, weight, once, twice):
    count, rows, width = weight.shape
    planes = x_planes(low, inner, high, down, up)
    weights = [down.at[2 * rows]] + [weight.at[x] for x in range(count)] + [up.at[2 * rows]]
    size = rows - 2
    before = slope(planes[1][1 : 1 + size] - planes[0][1 : 1 + size])
    for i in range(1, count + 3):
        fresh, before = update(planes, i, 1, size, before, weights[i - 1][1 : 1 + size])
        once[i - 1] = fresh
    planes = [once.at[i] for i in range(count + 2)]
    size = rows - 4
    before = slope(planes[1][1 : 1 + size] - planes[0][1 : 1 + size])
    for i in range(1, count + 1):
        fresh, before = update(planes, i, 1, size, before, weight[i - 1, 2 : 2 + size])
        for y in range(size):
            twice[:, i - 1, 2 + y] = fresh[y]


def smooth_middle(low, inner, high, down, up, tv_weight):
    count, rows, width = tv_weight.shape
    rank = low.shape[1]
    vmem = pl.BlockSpec(memory_space=pltpu.VMEM)
    return pl.pallas_call(
        smooth_middle_kernel,
        out_shape=(
            jax.ShapeDtypeStruct((count + 2, rows - 2, rank, width), jnp.float32),
            jax.ShapeDtypeStruct((rank, count, rows, width), jnp.float32),
        ),
        in_specs=[vmem] * 6,
        out_specs=(vmem,) * 2,
        compiler_params=pltpu.CompilerParams(vmem_limit_bytes=limit),
        cost_estimate=pl.CostEstimate(flops=50000000, bytes_accessed=3000000, transcendentals=1000000),
        name="smooth_middle",
    )(low, inner, high, down, up, tv_weight)


def smooth_edges_kernel(low, inner, high, down, up, left, right, once, twice, weight, out, field, fresher):
    count, rows, width = weight.shape
    planes = x_planes(low, inner, high, down, up)
    last = len(planes) - 1
    out[...] = twice[...]
    for side, received in enumerate((left, right)):
        edge = 1 if side else 2
        mine, theirs, shift = (0, 2, 2) if side else (2, 0, 0)
        outer = rows - 1 if side else 0
        own = slice(rows - 2, rows) if side else slice(0, 2)
        cells = [field.at[side, i] for i in range(last + 1)]
        for i in range(last + 1):
            cells[i][mine : mine + 2] = planes[i][own]
        for x in range(count):
            for y in range(2):
                cells[x + 2][theirs + y] = received[y * count + x]
        cells[1][3 - edge] = received[2 * count + 1]
        cells[last - 1][3 - edge] = received[2 * count + 2]
        before = slope(cells[1][edge : edge + 1] - cells[0][edge : edge + 1])
        fresh, _ = update(cells, 1, edge, 1, before, down[2 * rows, outer : outer + 1])
        fresher[side, 0, shift + edge - 1] = fresh[0]
        near = received[2 * count, :count][:, None, :]
        pair = [weight[:, outer : outer + 1], near]
        pair = jnp.concatenate(pair if side else pair[::-1], axis=1)
        fresher[side, 1 : count + 1, shift : shift + 2] = update_planes(field.at[side], 2, count, pair)
        before = slope(cells[last - 1][edge : edge + 1] - cells[last - 2][edge : edge + 1])
        fresh, _ = update(cells, last - 1, edge, 1, before, up[2 * rows, outer : outer + 1])
        fresher[side, count + 1, shift + edge - 1] = fresh[0]
        done = slice(rows - 4, rows - 2) if side else slice(0, 2)
        cells = [fresher.at[side, i] for i in range(count + 2)]
        for i in range(count + 2):
            cells[i][2 - shift : 4 - shift] = once[i, done]
        fresh = update_planes(fresher.at[side], 1, count, weight[:, own])
        for x in range(count):
            for y in range(2):
                out[:, x, own.start + y] = fresh[x, y]


def smooth_edges(low, inner, high, down, up, left, right, once, twice, tv_weight):
    count, rows, width = tv_weight.shape
    rank = low.shape[1]
    vmem = pl.BlockSpec(memory_space=pltpu.VMEM)
    return pl.pallas_call(
        smooth_edges_kernel,
        out_shape=jax.ShapeDtypeStruct((rank, count, rows, width), jnp.float32),
        in_specs=[vmem] * 10,
        out_specs=vmem,
        scratch_shapes=[
            pltpu.VMEM((2, count + 4, 4, rank, width), jnp.float32),
            pltpu.VMEM((2, count + 2, 4, rank, width), jnp.float32),
        ],
        compiler_params=pltpu.CompilerParams(vmem_limit_bytes=limit),
        name="smooth_edges",
    )(low, inner, high, down, up, left, right, once, twice, tv_weight)


def neighbours(axis, toward_low, toward_high):
    ends = lax.axis_size(axis) - 1
    return (
        lax.ppermute(toward_high, axis, [(i, i + 1) for i in range(ends)]),
        lax.ppermute(toward_low, axis, [(i + 1, i) for i in range(ends)]),
    )


def neighbours_in_pairs(axis, gap, chip):
    count = lax.axis_size(axis)
    between = [(i, i + 1) for i in range(1, count - 1, 2)]
    return (
        lax.ppermute(gap, axis, between + [(j, i) for i, j in between]),
        lax.ppermute(chip, axis, [(i, i ^ 1) for i in range(count)]),
    )


def on_device(signals, tile_flags, basis_old, tv_weight):
    frames, size_x, size_y, size_z = signals.shape
    rank = basis_old.shape[1]
    flags = jnp.transpose(tile_flags, (0, 2, 1))
    pinned = [pltpu.with_memory_space_constraint(a, pltpu.HBM) for a in (signals, flags, basis_old.T)]
    parts, kept = local_grown(*pinned, lax.axis_size("dev"))
    parts = lax.all_to_all(parts, "dev", 0, 0)
    summed = jnp.sum(parts, axis=0)
    parts = jnp.broadcast_to(summed[None], (lax.axis_size("grp"),) + summed.shape)
    parts = lax.all_to_all(parts, "grp", 0, 0)
    basis, mixer, low, high, even = project_outer(parts, kept, flags, tv_weight, rank)
    down, up = neighbours("grp", low, high)
    inner, chip, gap = project_inner(pinned[0], mixer, flags, tv_weight, low, high)
    heads = jnp.stack([down[size_y], up[0]])
    tails = jnp.stack([down[2 * size_y - 1], up[size_y - 1]])
    chip = jnp.concatenate([chip, jnp.where(even != 0, tails, heads)], axis=0)
    gap = jnp.concatenate([gap, jnp.where(even != 0, heads, tails)], axis=0)
    gap, chip = neighbours_in_pairs("dev", gap, chip)
    once, twice = smooth_middle(low, inner, high, down, up, tv_weight)
    left = jnp.where(even == 0, chip, gap)
    right = jnp.where(even == 0, gap, chip)
    return (basis.T, smooth_edges(low, inner, high, down, up, left, right, once, twice, tv_weight))


def solution(mesh):
    placed = (P(None, "grp", "dev", None), P("grp", "dev", None), P(), P("grp", "dev", None))
    return jax.shard_map(
        on_device,
        mesh=mesh,
        in_specs=placed,
        out_specs=(P(), P(None, "grp", "dev", None)),
        check_vma=False,
    )
```
